32 devices in a mesh: tile: 16 (over z, x, core), chan: 2 (over y).
Axes of the slice: x: 2, y: 2, z: 4, core: 2. Of those that a mesh axis runs over, the one named last changes fastest.
Arguments:
- analysis: bfloat16 [64, 131072], P('chan', 'tile'), may hold values from -6 to 6
- send_rows: int32 [16, 5, 128], P('tile'), may hold values from 0 to 8191
- send_count: int32 [16, 5], P('tile'), may hold values from 64 to 128, as said below
- corner_slot: int32 [4, 512, 256], P(None, 'tile'), may hold values from 0 to 639, as said below
- corner_weight: float32 [4, 512, 256], P(None, 'tile'), may hold values from 0.1 to 0.6
- beside: int32 [512, 8], P('tile'), may hold values from 0 to 511, as said below
- quarter_turns: int32 [512, 8], P('tile'), may hold values from 0 to 3
- kernel_one: bfloat16 [9, 128, 64], P(None, 'chan'), may hold values from -0.375 to 0.375
- kernel_two: bfloat16 [9, 128, 128], P(None, 'chan'), may hold values from -0.25 to 0.25
- kernel_three: bfloat16 [9, 128, 128], P(None, 'chan'), may hold values from -0.25 to 0.25
Outputs:
- forecast: bfloat16 [128, 512, 256], P('chan', 'tile')
The draws below stay inside these ranges and needn't reach their ends.
Inputs may be any that keep to these rules, and one draw needn't show every extreme that they name: send_count[s, d] is at least 64; every shard sends 128 to itself (d = 2), and some receiver gets 128 from each of its 5 senders. corner_slot[j, t, i] = d * 128 + k names a live slot, k < send_count[s, d], of the block that shard s = (e - d + 2) mod the shard count sends to the shard e holding tile t; the four corners of a pixel are slots k, k + 1, k + 2, k + 3 of one block. beside[t, k] = (t + d) mod 512 with 1 <= |d| <= 2.
All inputs are finite; a program needn't handle non-finite values.
Results may differ from the reference program's by a relative error of at most 0.007.
Values may be sent and summed in bfloat16 or wider, within the bound.
A program may use at most 64 MiB of HBM per device.

```python
import jax
import jax.numpy as jnp
import numpy as np
from jax import lax

CIN = 64
COUT = 128
P_SIZE = 16
PP = 256
TILE_DEV = 32
TILES = 512
LL_DEV = 8192
LL = 131072
CAP = 128
REACH = 2
NEAR = 5
N_TILE = 16


def receive_loads(key):
    shards = TILES // TILE_DEV
    near_count = 2 * REACH + 1
    folded = jax.random.fold_in(key, 71)
    counts = jax.random.randint(jax.random.fold_in(folded, 2), (shards, near_count), CAP // 2, CAP + 1)
    full_one = jax.random.randint(jax.random.fold_in(folded, 3), (), 0, shards)
    row_ids = jnp.arange(shards)[:, None]
    col_ids = jnp.arange(near_count)[None, :]
    counts = jnp.where(row_ids == full_one, CAP, counts)
    counts = jnp.where(col_ids == REACH, CAP, counts)
    return counts.astype(jnp.int32)


def draw_send_count(key, part):
    shards = TILES // TILE_DEV
    near_count = 2 * REACH + 1
    received = receive_loads(key)
    target = jnp.remainder(jnp.arange(shards)[:, None] + jnp.arange(near_count)[None, :] - REACH, shards)
    return received[target, jnp.arange(near_count)[None, :]].astype(jnp.int32)


def draw_corner_slot(key, part):
    shards = TILES // TILE_DEV
    received = receive_loads(key)
    upper_edge = jnp.cumsum(received, axis=1)
    lower_edge = upper_edge - received
    totals = upper_edge[:, -1]
    span = TILE_DEV * PP
    picked = jax.random.randint(jax.random.fold_in(key, 5), (shards, span), 0, totals[:, None])
    position = jnp.arange(span)[None, :]
    picked = jnp.where(position == 0, totals[:, None] - 1, picked)
    picked = jnp.where(position == 1, 0, picked)
    block = jnp.sum((picked[:, :, None] >= upper_edge[:, None, :]).astype(jnp.int32), axis=2)
    low_start = jnp.take_along_axis(lower_edge, block, axis=1)
    block_count = jnp.take_along_axis(received, block, axis=1)
    first_slot = jnp.minimum(picked - low_start, block_count - 4)
    corners = jnp.stack([block * CAP + first_slot + j for j in range(4)], axis=0)
    return corners.reshape(4, TILES, PP).astype(jnp.int32)


def draw_beside(key, part):
    steps_away = jax.random.randint(jax.random.fold_in(key, 31), (TILES, 8), 1, REACH + 1)
    flipped = jax.random.randint(jax.random.fold_in(key, 32), (TILES, 8), 0, 2)
    offset = jnp.where(flipped == 1, -steps_away, steps_away)
    offset = offset.at[0, 2].set(-1).at[TILES - 1, 3].set(1)
    return jnp.remainder(jnp.arange(TILES)[:, None] + offset, TILES).astype(jnp.int32)


def place_ends(values, rng, low, high):
    dims = values.shape
    index_at = [jax.random.randint(jax.random.fold_in(rng, axis), (), 0, dims[axis]) for axis in range(len(dims))]
    values = values.at[tuple(index_at)].set(low)
    longest = dims.index(max(dims))
    index_at[longest] = (index_at[longest] + 1) % dims[longest]
    return values.at[tuple(index_at)].set(high)


def block_levels(rng, shape, cuts, smallest, high):
    gain = 1.0
    for dim, shards_of in cuts:
        heights = jax.random.uniform(jax.random.fold_in(jax.random.fold_in(rng, 6), dim), (shards_of,), jnp.float32, smallest / len(cuts), high / len(cuts))
        gain = gain * jnp.repeat(jnp.exp(heights), shape[dim] // shards_of).reshape((-1,) + (1,) * (len(shape) - 1 - dim))
    return gain


def gaussian(rng, shape, width, bound, pieces=(), held_as=jnp.bfloat16):
    values = jax.random.normal(rng, shape, jnp.float32) * width
    if len(pieces) > 0:
        values = block_levels(rng, shape, pieces, -0.22, 0.18) * values
    return jnp.clip(values, min=-bound, max=bound).astype(held_as)


def setup_inputs(seed: int = 0) -> dict:
    streams_of = jax.random.split(jax.random.key(seed), 11)
    return {
        "analysis": gaussian(streams_of[0], (CIN, LL), 1.0, 6.0, ((0, 2), (1, 16))),
        "send_rows": place_ends(jax.random.randint(streams_of[1], (N_TILE, NEAR, CAP), 0, LL_DEV), jax.random.fold_in(streams_of[1], 1), 0, LL_DEV - 1).astype(jnp.int32),
        "send_count": draw_send_count(jax.random.fold_in(streams_of[10], 71), 0),
        "corner_slot": draw_corner_slot(jax.random.fold_in(streams_of[10], 71), 0),
        "corner_weight": jnp.clip(0.1 + 0.5 * jax.random.uniform(streams_of[4], (4, TILES, PP), jnp.float32) ** block_levels(streams_of[4], (4, TILES, PP), ((1, 16),), -0.2, 0.2), 0.1, 0.6),
        "beside": draw_beside(jax.random.fold_in(streams_of[10], 71), 0),
        "quarter_turns": place_ends(jax.random.randint(streams_of[6], (TILES, 8), 0, 4), jax.random.fold_in(streams_of[6], 1), 0, 3).astype(jnp.int32),
        "kernel_one": gaussian(streams_of[7], (9, COUT, CIN), (9 * CIN // 2) ** -0.5, 0.375, ((1, 2),)),
        "kernel_two": gaussian(streams_of[8], (9, COUT, COUT), (9 * COUT // 2) ** -0.5, 0.25, ((1, 2),)),
        "kernel_three": gaussian(streams_of[9], (9, COUT, COUT), (9 * COUT // 2) ** -0.5, 0.25, ((1, 2),)),
    }


def cycle_table(extent):
    length = 4 * extent - 4
    entries = []
    for cycle_pos in range(length):
        if cycle_pos < extent:
            row_at, col_at = cycle_pos, 0
        elif cycle_pos < 2 * extent - 1:
            row_at, col_at = extent - 1, cycle_pos - extent + 1
        elif cycle_pos < 3 * extent - 2:
            row_at, col_at = 3 * extent - 3 - cycle_pos, extent - 1
        else:
            row_at, col_at = 0, 4 * extent - 4 - cycle_pos
        entries.append(row_at * extent + col_at)
    return np.array(entries, np.int32)


def border_tables(extent):
    length = 4 * extent - 4
    heading = []
    anchor = []
    for col_at in range(extent):
        heading.append(0)
        anchor.append(extent - 1 + col_at)
    for col_at in range(extent):
        heading.append(1)
        anchor.append((length - col_at) % length)
    for row_at in range(extent):
        heading.append(2)
        anchor.append(3 * extent - 3 - row_at)
    for row_at in range(extent):
        heading.append(3)
        anchor.append(row_at)
    heading += [4, 5, 6, 7]
    anchor += [2 * extent - 2, extent - 1, 3 * extent - 3, 0]
    return np.array(heading, np.int32), np.array(anchor, np.int32)


def layout_table(extent):
    padded_side = extent + 2
    interior = extent * extent
    entries = []
    for row_at in range(padded_side):
        for col_at in range(padded_side):
            if 1 <= row_at <= extent and 1 <= col_at <= extent:
                entries.append((row_at - 1) * extent + col_at - 1)
            elif row_at == 0 and 1 <= col_at <= extent:
                entries.append(interior + col_at - 1)
            elif row_at == padded_side - 1 and 1 <= col_at <= extent:
                entries.append(interior + extent + col_at - 1)
            elif col_at == 0 and 1 <= row_at <= extent:
                entries.append(interior + 2 * extent + row_at - 1)
            elif col_at == padded_side - 1 and 1 <= row_at <= extent:
                entries.append(interior + 3 * extent + row_at - 1)
            else:
                corner = (0 if row_at == 0 else 2) + (0 if col_at == 0 else 1)
                entries.append(interior + 4 * extent + corner)
    return np.array(entries, np.int32)


def border_values(cycle_vals, neighbours, rotations):
    heading, anchor = border_tables(P_SIZE)
    length = 4 * P_SIZE - 4
    near_tile = jnp.take(neighbours, heading, axis=1)
    near_turn = jnp.take(rotations, heading, axis=1)
    source = near_tile * length + jnp.remainder(anchor[None, :] - near_turn * (P_SIZE - 1), length)
    flat_cycles = cycle_vals.reshape(cycle_vals.shape[0], -1)
    picked = jnp.take(flat_cycles, source.reshape(-1), axis=1)
    return picked.reshape(cycle_vals.shape[0], neighbours.shape[0], 4 * P_SIZE + 4)


def stencil(padded, kernel):
    padded_side = P_SIZE + 2
    stretch = P_SIZE * padded_side - 2
    summed = jnp.zeros((kernel.shape[1], padded.shape[1], stretch), jnp.float32)
    for tap_index in range(9):
        offset = padded_side + 1 + (tap_index // 3 - 1) * padded_side + (tap_index % 3 - 1)
        window = padded[:, :, offset:offset + stretch].astype(jnp.float32)
        summed = summed + jnp.einsum('oc,ctq->otq', kernel[tap_index].astype(jnp.float32), window)
    summed = jnp.pad(summed, ((0, 0), (0, 0), (0, 2)))
    summed = summed.reshape(summed.shape[0], summed.shape[1], P_SIZE, padded_side)[:, :, :, :P_SIZE]
    summed = summed.reshape(summed.shape[0], summed.shape[1], P_SIZE * P_SIZE)
    return jax.nn.gelu(summed, approximate=False).astype(jnp.bfloat16)


def conv_all(activity, kernel, beside, quarter_turns):
    cycle_vals = jnp.take(activity, cycle_table(P_SIZE), axis=2)
    border = border_values(cycle_vals, beside, quarter_turns)
    joined = jnp.concatenate([activity, border], axis=2)
    padded = jnp.take(joined, layout_table(P_SIZE), axis=2)
    blocks = padded.reshape(padded.shape[0], TILES // TILE_DEV, TILE_DEV, padded.shape[2])
    blocks = jnp.transpose(blocks, (1, 0, 2, 3))
    result = lax.map(lambda block: stencil(block, kernel), blocks)
    return jnp.transpose(result, (1, 0, 2, 3)).reshape(kernel.shape[1], TILES, PP)


def reference(analysis, send_rows, send_count, corner_slot, corner_weight, beside, quarter_turns, kernel_one, kernel_two, kernel_three):
    shards = TILES // TILE_DEV
    slot_blocks = corner_slot.reshape(4, shards, TILE_DEV * PP)
    weight_blocks = corner_weight.reshape(4, shards, TILE_DEV * PP)

    def one_shard(receiver):
        slot_ids = jnp.take(slot_blocks, receiver, axis=1)
        weights = jnp.take(weight_blocks, receiver, axis=1)
        offset_index = slot_ids // CAP
        slot_index = slot_ids % CAP
        source = jnp.remainder(receiver - offset_index + REACH, shards).astype(jnp.int32)
        rows_sent = send_rows[source, offset_index, slot_index]
        is_live = slot_index < send_count[source, offset_index]
        point_index = (source * LL_DEV + rows_sent).astype(jnp.int32)
        values = jnp.take(analysis, point_index.reshape(-1), axis=1).reshape(CIN, 4, TILE_DEV * PP)
        values = jnp.where(is_live[None], values.astype(jnp.float32), jnp.float32(0.0))
        return jnp.sum(values * weights[None], axis=1).astype(jnp.bfloat16)

    receivers = jnp.arange(shards).astype(jnp.int32)
    regridded = lax.map(one_shard, receivers)
    regridded = jnp.transpose(regridded, (1, 0, 2)).reshape(CIN, TILES, PP)
    first = conv_all(regridded, kernel_one, beside, quarter_turns)
    second = conv_all(first, kernel_two, beside, quarter_turns)
    return conv_all(second, kernel_three, beside, quarter_turns)
```

```python
import jax
import jax.numpy as jnp
import numpy as np
from jax import lax
from jax.sharding import PartitionSpec as P

P_SIZE = 16
REACH = 2
LAYERS = 3


def from_behind(value, axis, steps):
    count = lax.axis_size(axis)
    pairs = [(source, (source + steps) % count) for source in range(count)]
    return lax.ppermute(value, axis, pairs)


def side_keys():
    extent = P_SIZE
    top = [-1] + [4 * extent - 4 - i for i in range(1, extent - 1)] + [-1]
    bottom = [-1] + [extent - 1 + i for i in range(1, extent)]
    left = list(range(extent))
    right = [3 * extent - 3 - i for i in range(extent - 1)] + [-1]
    one = np.array(top + bottom + left + right, np.int32)
    return np.concatenate([np.where(one < 0, -1, one + k * 64) for k in range(2 * REACH + 1)])


def border_tables():
    extent = P_SIZE
    length = 4 * extent - 4
    entries = [(4, 2 * extent - 2)] + [(0, extent - 1 + i) for i in range(extent)] + [(5, extent - 1)]
    entries += [(6, 3 * extent - 3)] + [(1, (length - i) % length) for i in range(extent)] + [(7, 0)]
    entries += [(2, 3 * extent - 3 - i) for i in range(extent)]
    entries += [(3, i) for i in range(extent)]
    heading, anchor = zip(*entries)
    return np.array(heading, np.int32), np.array(anchor, np.int32)


def widened(x, width, axes):
    length = x.shape[0]
    before, after = [], []
    left = width
    hop = 1
    while left > 0:
        n = min(left, length)
        before.insert(0, from_behind(x[length - n :], axes, hop))
        after.append(from_behind(x[:n], axes, -hop))
        left -= n
        hop += 1
    return jnp.concatenate(before + [x] + after, axis=0)


def conv_layer(x, kernel, select):
    tiles = x.shape[0] - 2 * REACH
    channels = x.shape[3]
    sides = jnp.concatenate([x[:, 0], x[:, P_SIZE - 1], x[:, :, 0], x[:, :, P_SIZE - 1]], axis=1)
    near = jnp.concatenate([sides[i : i + tiles] for i in range(2 * REACH + 1)], axis=1)
    border = jnp.einsum("tbs,tsc->tbc", select, near, preferred_element_type=jnp.float32).astype(jnp.bfloat16)
    side = P_SIZE + 2
    above = border[:, :side].reshape(tiles, 1, side, channels)
    below = border[:, side : 2 * side].reshape(tiles, 1, side, channels)
    left = border[:, 2 * side : 2 * side + P_SIZE].reshape(tiles, P_SIZE, 1, channels)
    right = border[:, 2 * side + P_SIZE :].reshape(tiles, P_SIZE, 1, channels)
    middle = jnp.concatenate([left, x[REACH : REACH + tiles], right], axis=2)
    padded = jnp.concatenate([above, middle, below], axis=1)
    summed = lax.conv_general_dilated(
        padded,
        kernel.reshape(3, 3, kernel.shape[1], kernel.shape[2]),
        (1, 1),
        "VALID",
        dimension_numbers=("NHWC", "HWOI", "NHWC"),
        preferred_element_type=jnp.float32,
    )
    return jax.nn.gelu(summed, approximate=False).astype(jnp.bfloat16)


def on_device(
    analysis,
    send_rows,
    send_count,
    corner_slot,
    corner_weight,
    beside,
    quarter_turns,
    kernel_one,
    kernel_two,
    kernel_three,
):
    shards = lax.axis_size("tile")
    groups = lax.axis_size("chan")
    both = ("tile", "chan")
    tiles_here = corner_slot.shape[1]
    pixels = corner_slot.shape[2]
    near_count, capacity = send_rows.shape[1:]
    total_tiles = tiles_here * shards
    per_group = tiles_here // groups
    mine = lax.axis_index("chan") * per_group
    first_tile = lax.axis_index("tile") * tiles_here + mine

    picked = jnp.take(analysis, send_rows.reshape(-1), axis=1, mode="clip")
    live = jnp.arange(capacity)[None, :] < send_count[0][:, None]
    picked = jnp.where(live.reshape(-1)[None, :], picked, jnp.zeros((), picked.dtype))
    blocks = []
    for d in range(near_count):
        piece = picked[:, d * capacity : (d + 1) * capacity]
        blocks.append(piece if d == REACH else from_behind(piece, "tile", d - REACH))
    arrived = jnp.concatenate(blocks, axis=1)
    arrived = lax.all_gather(arrived, "chan", axis=0, tiled=True)

    sizes = [k.shape[2] for k in (kernel_one, kernel_two, kernel_three)]
    joined = jnp.concatenate([kernel_one, kernel_two, kernel_three], axis=2)
    joined = lax.all_gather(joined, "chan", axis=1, tiled=True)
    cuts = np.cumsum([0] + sizes)
    kernels = [joined[:, :, cuts[i] : cuts[i + 1]] for i in range(LAYERS)]

    near = lax.dynamic_slice_in_dim(beside * 4 + quarter_turns, mine, per_group, 0)
    wide = REACH * (LAYERS - 1)
    near = widened(near, wide, both)
    tile_ids = first_tile - wide + jnp.arange(near.shape[0])
    steps = jnp.remainder(near // 4 - tile_ids[:, None] + REACH, total_tiles)
    turns = near % 4
    heading, anchor = border_tables()
    near_step = jnp.stack([steps[:, k] for k in heading], axis=1)
    near_turn = jnp.stack([turns[:, k] for k in heading], axis=1)
    source = near_step * 64 + jnp.remainder(anchor[None, :] - near_turn * (P_SIZE - 1), 4 * P_SIZE - 4)
    select = (source[:, :, None] == side_keys()[None, None, :]).astype(jnp.bfloat16)

    base = lax.dynamic_slice_in_dim(corner_slot[0], mine, per_group, 0).reshape(-1)
    weights = lax.dynamic_slice_in_dim(corner_weight, mine, per_group, 1).reshape(4, -1)
    away = jnp.arange(near_count * capacity)[:, None] - base[None, :]
    coarse = lax.reduce_precision(weights, 8, 7)
    x = jnp.zeros((), jnp.float32)
    for part in (coarse, weights - coarse):
        part = part.astype(jnp.bfloat16)
        spread = jnp.zeros((), jnp.bfloat16)
        for j in range(4):
            spread = jnp.where(away == j, part[j][None, :], spread)
        x = x + lax.dot_general(spread, arrived, (((0,), (1,)), ((), ())), preferred_element_type=jnp.float32)
    x = x.astype(jnp.bfloat16).reshape(per_group, P_SIZE, P_SIZE, arrived.shape[0])

    x = widened(x, REACH * LAYERS, both)
    for i in range(LAYERS):
        out = per_group + 2 * REACH * (LAYERS - 1 - i)
        cut = REACH * i
        x = conv_layer(x, kernels[i], select[cut : cut + out])
    x = jnp.transpose(x.reshape(per_group, pixels, x.shape[3]), (2, 0, 1))
    return lax.all_to_all(x, "chan", split_axis=0, concat_axis=1, tiled=True)


def solution(mesh):
    return jax.shard_map(
        on_device,
        mesh=mesh,
        in_specs=(
            P("chan", "tile"),
            P("tile", None, None),
            P("tile", None),
            P(None, "tile", None),
            P(None, "tile", None),
            P("tile", None),
            P("tile", None),
            P(None, "chan", None),
            P(None, "chan", None),
            P(None, "chan", None),
        ),
        out_specs=P("chan", "tile", None),
        check_vma=False,
    )
```

```python
import jax
import jax.numpy as jnp
import numpy as np
from jax import lax
from jax.sharding import PartitionSpec as P

P_SIZE = 16
REACH = 2
LAYERS = 3


def from_behind(value, axis, steps):
    count = lax.axis_size(axis)
    pairs = [(source, (source + steps) % count) for source in range(count)]
    return lax.ppermute(value, axis, pairs)


def side_keys():
    extent = P_SIZE
    top = [-1] + [4 * extent - 4 - i for i in range(1, extent - 1)] + [-1]
    bottom = [-1] + [extent - 1 + i for i in range(1, extent)]
    left = list(range(extent))
    right = [3 * extent - 3 - i for i in range(extent - 1)] + [-1]
    one = np.array(top + bottom + left + right, np.int32)
    return np.concatenate([np.where(one < 0, -1, one + k * 64) for k in range(2 * REACH + 1)])


def border_tables():
    extent = P_SIZE
    length = 4 * extent - 4
    entries = [(4, 2 * extent - 2)] + [(0, extent - 1 + i) for i in range(extent)] + [(5, extent - 1)]
    entries += [(6, 3 * extent - 3)] + [(1, (length - i) % length) for i in range(extent)] + [(7, 0)]
    entries += [(2, 3 * extent - 3 - i) for i in range(extent)]
    entries += [(3, i) for i in range(extent)]
    heading, anchor = zip(*entries)
    return np.array(heading, np.int32), np.array(anchor, np.int32)


def around(x, width, axes):
    length = x.shape[0]
    before, after = [], []
    left = width
    hop = 1
    while left > 0:
        n = min(left, length)
        before.insert(0, from_behind(x[length - n :], axes, hop))
        after.append(from_behind(x[:n], axes, -hop))
        left -= n
        hop += 1
    return jnp.concatenate(before, axis=0), jnp.concatenate(after, axis=0)


def gathered(x, axis, dim):
    if lax.axis_size(axis) != 2:
        return lax.all_gather(x, axis, axis=dim, tiled=True)
    other = lax.ppermute(x, axis, [(0, 1), (1, 0)])
    first = lax.axis_index(axis) == 0
    low, high = jnp.where(first, x, other), jnp.where(first, other, x)
    return jnp.concatenate([low, high], axis=dim)


def with_rims(x, select):
    tiles = x.shape[0] - 2 * REACH
    channels = x.shape[3]
    sides = jnp.concatenate([x[:, 0], x[:, P_SIZE - 1], x[:, :, 0], x[:, :, P_SIZE - 1]], axis=1)
    near = jnp.concatenate([sides[i : i + tiles] for i in range(2 * REACH + 1)], axis=1)
    border = jnp.einsum("tbs,tsc->tbc", select, near, preferred_element_type=jnp.float32).astype(jnp.bfloat16)
    side = P_SIZE + 2
    above = border[:, :side].reshape(tiles, 1, side, channels)
    below = border[:, side : 2 * side].reshape(tiles, 1, side, channels)
    left = border[:, 2 * side : 2 * side + P_SIZE].reshape(tiles, P_SIZE, 1, channels)
    right = border[:, 2 * side + P_SIZE :].reshape(tiles, P_SIZE, 1, channels)
    middle = jnp.concatenate([left, x[REACH : REACH + tiles], right], axis=2)
    return jnp.concatenate([above, middle, below], axis=1)


def conv(padded, kernel):
    summed = lax.conv_general_dilated(
        padded,
        kernel.reshape(3, 3, kernel.shape[1], kernel.shape[2]),
        (1, 1),
        "VALID",
        dimension_numbers=("NHWC", "HWOI", "NHWC"),
        preferred_element_type=jnp.float32,
    )
    return jax.nn.gelu(summed, approximate=False).astype(jnp.bfloat16)


def on_device(
    analysis,
    send_rows,
    send_count,
    corner_slot,
    corner_weight,
    beside,
    quarter_turns,
    kernel_one,
    kernel_two,
    kernel_three,
):
    shards = lax.axis_size("tile")
    groups = lax.axis_size("chan")
    both = ("tile", "chan")
    tiles_here = corner_slot.shape[1]
    pixels = corner_slot.shape[2]
    near_count, capacity = send_rows.shape[1:]
    total_tiles = tiles_here * shards
    per_group = tiles_here // groups
    mine = lax.axis_index("chan") * per_group
    first_tile = lax.axis_index("tile") * tiles_here + mine

    picked = jnp.take(analysis, send_rows.reshape(-1), axis=1, mode="clip")
    live = jnp.arange(capacity)[None, :] < send_count[0][:, None]
    picked = jnp.where(live.reshape(-1)[None, :], picked, jnp.zeros((), picked.dtype))
    blocks = []
    for d in range(near_count):
        piece = picked[:, d * capacity : (d + 1) * capacity]
        blocks.append(piece if d == REACH else from_behind(piece, "tile", d - REACH))
    arrived = jnp.concatenate(blocks, axis=1)
    arrived = gathered(arrived, "chan", 0)

    sizes = [k.shape[2] for k in (kernel_one, kernel_two, kernel_three)]
    joined = jnp.concatenate([kernel_one, kernel_two, kernel_three], axis=2)
    joined = gathered(joined, "chan", 1)
    cuts = np.cumsum([0] + sizes)
    kernels = [joined[:, :, cuts[i] : cuts[i + 1]] for i in range(LAYERS)]

    near = lax.dynamic_slice_in_dim(beside * 4 + quarter_turns, mine, per_group, 0)
    wide = REACH * (LAYERS - 1)
    early, late = around(near, wide, both)
    near = jnp.concatenate([early, near, late], axis=0)
    tile_ids = first_tile - wide + jnp.arange(near.shape[0])
    steps = jnp.remainder(near // 4 - tile_ids[:, None] + REACH, total_tiles)
    turns = near % 4
    heading, anchor = border_tables()
    near_step = jnp.stack([steps[:, k] for k in heading], axis=1)
    near_turn = jnp.stack([turns[:, k] for k in heading], axis=1)
    source = near_step * 64 + jnp.remainder(anchor[None, :] - near_turn * (P_SIZE - 1), 4 * P_SIZE - 4)
    select = (source[:, :, None] == side_keys()[None, None, :]).astype(jnp.bfloat16)

    base = lax.dynamic_slice_in_dim(corner_slot[0], mine, per_group, 0).reshape(-1)
    weights = lax.dynamic_slice_in_dim(corner_weight, mine, per_group, 1).reshape(4, -1)
    away = jnp.arange(near_count * capacity)[:, None] - base[None, :]
    coarse = lax.reduce_precision(weights, 8, 7)
    x = jnp.zeros((), jnp.float32)
    for part in (coarse, weights - coarse):
        part = part.astype(jnp.bfloat16)
        spread = jnp.zeros((), jnp.bfloat16)
        for j in range(4):
            spread = jnp.where(away == j, part[j][None, :], spread)
        x = x + lax.dot_general(spread, arrived, (((0,), (1,)), ((), ())), preferred_element_type=jnp.float32)
    x = x.astype(jnp.bfloat16).reshape(per_group, P_SIZE, P_SIZE, arrived.shape[0])

    width, reach = REACH * LAYERS, 2 * REACH
    early, late = around(x, width, both)
    if per_group > reach:
        inner = conv(with_rims(x, select[width : width + per_group - reach]), kernels[0])
        edges = [
            with_rims(jnp.concatenate([early, x[:reach]], axis=0), select[:width]),
            with_rims(jnp.concatenate([x[per_group - reach :], late], axis=0), select[select.shape[0] - width :]),
        ]
        outer = conv(jnp.concatenate(edges, axis=0), kernels[0])
        x = jnp.concatenate([outer[:width], inner, outer[width:]], axis=0)
    else:
        x = conv(with_rims(jnp.concatenate([early, x, late], axis=0), select), kernels[0])
    x = conv(with_rims(x, select[REACH : REACH + per_group + reach]), kernels[1])
    padded = with_rims(x, select[reach : reach + per_group])

    def last(block):
        y = conv(block, kernels[2])
        return jnp.transpose(y.reshape(y.shape[0], pixels, y.shape[3]), (2, 0, 1))

    if groups != 2:
        return lax.all_to_all(last(padded), "chan", split_axis=0, concat_axis=1, tiled=True)
    first = lax.axis_index("chan") == 0
    kept, came = [], []
    half = per_group // 2
    for start in range(0, per_group, half):
        y = last(padded[start : start + half])
        share = y.shape[0] // 2
        kept.append(jnp.where(first, y[:share], y[share:]))
        came.append(lax.ppermute(jnp.where(first, y[share:], y[:share]), "chan", [(0, 1), (1, 0)]))
    kept, came = jnp.concatenate(kept, axis=1), jnp.concatenate(came, axis=1)
    return jnp.concatenate([jnp.where(first, kept, came), jnp.where(first, came, kept)], axis=1)


def solution(mesh):
    return jax.shard_map(
        on_device,
        mesh=mesh,
        in_specs=(
            P("chan", "tile"),
            P("tile", None, None),
            P("tile", None),
            P(None, "tile", None),
            P(None, "tile", None),
            P("tile", None),
            P("tile", None),
            P(None, "chan", None),
            P(None, "chan", None),
            P(None, "chan", None),
        ),
        out_specs=P("chan", "tile", None),
        check_vma=False,
    )
```

```python
import jax
import jax.numpy as jnp
import numpy as np
from jax import lax
from jax.sharding import PartitionSpec as P

P_SIZE = 16
REACH = 2
LAYERS = 3


def from_behind(value, axis, steps):
    count = lax.axis_size(axis)
    pairs = [(source, (source + steps) % count) for source in range(count)]
    return lax.ppermute(value, axis, pairs)


def side_keys():
    extent = P_SIZE
    top = [-1] + [4 * extent - 4 - i for i in range(1, extent - 1)] + [-1]
    bottom = [-1] + [extent - 1 + i for i in range(1, extent)]
    left = list(range(extent))
    right = [3 * extent - 3 - i for i in range(extent - 1)] + [-1]
    one = np.array(top + bottom + left + right, np.int32)
    return np.concatenate([np.where(one < 0, -1, one + k * 64) for k in range(2 * REACH + 1)])


def border_tables():
    extent = P_SIZE
    length = 4 * extent - 4
    entries = [(4, 2 * extent - 2)] + [(0, extent - 1 + i) for i in range(extent)] + [(5, extent - 1)]
    entries += [(6, 3 * extent - 3)] + [(1, (length - i) % length) for i in range(extent)] + [(7, 0)]
    entries += [(2, 3 * extent - 3 - i) for i in range(extent)]
    entries += [(3, i) for i in range(extent)]
    heading, anchor = zip(*entries)
    return np.array(heading, np.int32), np.array(anchor, np.int32)


def around(x, width, axes):
    length = x.shape[0]
    before, after = [], []
    left = width
    hop = 1
    while left > 0:
        n = min(left, length)
        before.insert(0, from_behind(x[length - n :], axes, hop))
        after.append(from_behind(x[:n], axes, -hop))
        left -= n
        hop += 1
    return jnp.concatenate(before, axis=0), jnp.concatenate(after, axis=0)


def gathered(x, axis, dim):
    if lax.axis_size(axis) != 2:
        return lax.all_gather(x, axis, axis=dim, tiled=True)
    other = lax.ppermute(x, axis, [(0, 1), (1, 0)])
    first = lax.axis_index(axis) == 0
    low, high = jnp.where(first, x, other), jnp.where(first, other, x)
    return jnp.concatenate([low, high], axis=dim)


def with_rims(x, select):
    tiles = x.shape[0] - 2 * REACH
    channels = x.shape[3]
    sides = jnp.concatenate([x[:, 0], x[:, P_SIZE - 1], x[:, :, 0], x[:, :, P_SIZE - 1]], axis=1)
    near = jnp.concatenate([sides[i : i + tiles] for i in range(2 * REACH + 1)], axis=1)
    border = jnp.einsum("tbs,tsc->tbc", select, near, preferred_element_type=jnp.float32).astype(jnp.bfloat16)
    side = P_SIZE + 2
    above = border[:, :side].reshape(tiles, 1, side, channels)
    below = border[:, side : 2 * side].reshape(tiles, 1, side, channels)
    left = border[:, 2 * side : 2 * side + P_SIZE].reshape(tiles, P_SIZE, 1, channels)
    right = border[:, 2 * side + P_SIZE :].reshape(tiles, P_SIZE, 1, channels)
    middle = jnp.concatenate([left, x[REACH : REACH + tiles], right], axis=2)
    return jnp.concatenate([above, middle, below], axis=1)


def conv(padded, kernel):
    summed = lax.conv_general_dilated(
        padded,
        kernel.reshape(3, 3, kernel.shape[1], kernel.shape[2]),
        (1, 1),
        "VALID",
        dimension_numbers=("NHWC", "HWOI", "NHWC"),
        preferred_element_type=jnp.float32,
    )
    return jax.nn.gelu(summed, approximate=False).astype(jnp.bfloat16)


def on_device(
    analysis,
    send_rows,
    send_count,
    corner_slot,
    corner_weight,
    beside,
    quarter_turns,
    kernel_one,
    kernel_two,
    kernel_three,
):
    shards = lax.axis_size("tile")
    groups = lax.axis_size("chan")
    both = ("tile", "chan")
    tiles_here = corner_slot.shape[1]
    pixels = corner_slot.shape[2]
    near_count, capacity = send_rows.shape[1:]
    total_tiles = tiles_here * shards
    per_group = tiles_here // groups
    mine = lax.axis_index("chan") * per_group

    picked = jnp.take(analysis, send_rows.reshape(-1), axis=1, mode="clip")
    live = jnp.arange(capacity)[None, :] < send_count[0][:, None]
    picked = jnp.where(live.reshape(-1)[None, :], picked, jnp.zeros((), picked.dtype))
    wide = REACH * (LAYERS - 1)
    tile_ids = lax.axis_index("tile") * tiles_here + jnp.arange(tiles_here)
    steps = jnp.remainder(beside - tile_ids[:, None] + REACH, total_tiles)
    near = steps * 4 + quarter_turns
    riders = {1: near[tiles_here - wide :], -1: near[:wide]}
    came_along = {}
    blocks = []
    for d in range(near_count):
        hop = d - REACH
        piece = picked[:, d * capacity : (d + 1) * capacity]
        if hop in riders:
            rider = riders[hop].astype(piece.dtype).reshape(piece.shape[0], -1)
            piece = from_behind(jnp.concatenate([piece, rider], axis=1), "tile", hop)
            came_along[hop] = piece[:, capacity:].reshape(wide, -1).astype(jnp.int32)
            piece = piece[:, :capacity]
        elif hop != 0:
            piece = from_behind(piece, "tile", hop)
        blocks.append(piece)
    arrived = gathered(jnp.concatenate(blocks, axis=1), "chan", 0)

    sizes = [k.shape[2] for k in (kernel_one, kernel_two, kernel_three)]
    joined = jnp.concatenate([kernel_one, kernel_two, kernel_three], axis=2)
    joined = gathered(joined, "chan", 1)
    cuts = np.cumsum([0] + sizes)
    kernels = [joined[:, :, cuts[i] : cuts[i + 1]] for i in range(LAYERS)]

    near = jnp.concatenate([came_along[1], near, came_along[-1]], axis=0)
    near = lax.dynamic_slice_in_dim(near, mine, per_group + 2 * wide, 0)
    steps, turns = near // 4, near % 4
    heading, anchor = border_tables()
    near_step = jnp.stack([steps[:, k] for k in heading], axis=1)
    near_turn = jnp.stack([turns[:, k] for k in heading], axis=1)
    source = near_step * 64 + jnp.remainder(anchor[None, :] - near_turn * (P_SIZE - 1), 4 * P_SIZE - 4)
    select = (source[:, :, None] == side_keys()[None, None, :]).astype(jnp.bfloat16)

    base = lax.dynamic_slice_in_dim(corner_slot[0], mine, per_group, 0).reshape(-1)
    weights = lax.dynamic_slice_in_dim(corner_weight, mine, per_group, 1).reshape(4, -1)
    away = jnp.arange(near_count * capacity)[:, None] - base[None, :]
    coarse = lax.reduce_precision(weights, 8, 7)
    x = jnp.zeros((), jnp.float32)
    for part in (coarse, weights - coarse):
        part = part.astype(jnp.bfloat16)
        spread = jnp.zeros((), jnp.bfloat16)
        for j in range(4):
            spread = jnp.where(away == j, part[j][None, :], spread)
        x = x + lax.dot_general(spread, arrived, (((0,), (1,)), ((), ())), preferred_element_type=jnp.float32)
    x = x.astype(jnp.bfloat16).reshape(per_group, P_SIZE, P_SIZE, arrived.shape[0])

    reach = 2 * REACH
    early, late = around(x, REACH * LAYERS, both)
    x = conv(with_rims(jnp.concatenate([early, x, late], axis=0), select), kernels[0])
    padded = with_rims(x, select[REACH : REACH + per_group + reach])

    def last(x, select):
        y = conv(with_rims(x, select), kernels[2])
        return jnp.transpose(y.reshape(y.shape[0], pixels, y.shape[3]), (2, 0, 1))

    select = select[reach : reach + per_group]
    if groups != 2:
        x = last(conv(padded, kernels[1]), select)
        return lax.all_to_all(x, "chan", split_axis=0, concat_axis=1, tiled=True)
    first = lax.axis_index("chan") == 0
    kept, came = [], []
    half = per_group // 2
    x = None
    for k in range(2):
        if k == 0:
            x = conv(padded[: half + reach], kernels[1])
        else:
            rest = conv(padded[half + reach :], kernels[1])
            x = jnp.concatenate([x[half:], rest], axis=0)
        y = last(x, select[k * half : (k + 1) * half])
        share = y.shape[0] // 2
        kept.append(jnp.where(first, y[:share], y[share:]))
        sent = jnp.where(first, y[share:], y[:share])
        if k == 0:
            sent, padded = lax.optimization_barrier((sent, padded))
        came.append(lax.ppermute(sent, "chan", [(0, 1), (1, 0)]))
    kept, came = jnp.concatenate(kept, axis=1), jnp.concatenate(came, axis=1)
    return jnp.concatenate([jnp.where(first, kept, came), jnp.where(first, came, kept)], axis=1)


def solution(mesh):
    return jax.shard_map(
        on_device,
        mesh=mesh,
        in_specs=(
            P("chan", "tile"),
            P("tile", None, None),
            P("tile", None),
            P(None, "tile", None),
            P(None, "tile", None),
            P("tile", None),
            P("tile", None),
            P(None, "chan", None),
            P(None, "chan", None),
            P(None, "chan", None),
        ),
        out_specs=P("chan", "tile", None),
        check_vma=False,
    )
```

```python
import jax
import jax.numpy as jnp
import numpy as np
from jax import lax
from jax.sharding import PartitionSpec as P

P_SIZE = 16
REACH = 2
LAYERS = 3


def from_behind(value, axis, steps):
    count = lax.axis_size(axis)
    pairs = [(source, (source + steps) % count) for source in range(count)]
    return lax.ppermute(value, axis, pairs)


def side_keys():
    extent = P_SIZE
    top = [-1] + [4 * extent - 4 - i for i in range(1, extent - 1)] + [-1]
    bottom = [-1] + [extent - 1 + i for i in range(1, extent)]
    left = list(range(extent))
    right = [3 * extent - 3 - i for i in range(extent - 1)] + [-1]
    one = np.array(top + bottom + left + right, np.int32)
    return np.concatenate([np.where(one < 0, -1, one + k * 64) for k in range(2 * REACH + 1)])


def border_tables():
    extent = P_SIZE
    length = 4 * extent - 4
    entries = [(4, 2 * extent - 2)] + [(0, extent - 1 + i) for i in range(extent)] + [(5, extent - 1)]
    entries += [(6, 3 * extent - 3)] + [(1, (length - i) % length) for i in range(extent)] + [(7, 0)]
    entries += [(2, 3 * extent - 3 - i) for i in range(extent)]
    entries += [(3, i) for i in range(extent)]
    heading, anchor = zip(*entries)
    return np.array(heading, np.int32), np.array(anchor, np.int32)


def around(x, width, axes):
    length = x.shape[0]
    before, after = [], []
    left = width
    hop = 1
    while left > 0:
        n = min(left, length)
        before.insert(0, from_behind(x[length - n :], axes, hop))
        after.append(from_behind(x[:n], axes, -hop))
        left -= n
        hop += 1
    return jnp.concatenate(before, axis=0), jnp.concatenate(after, axis=0)


def gathered(x, axis, dim):
    if lax.axis_size(axis) != 2:
        return lax.all_gather(x, axis, axis=dim, tiled=True)
    other = lax.ppermute(x, axis, [(0, 1), (1, 0)])
    first = lax.axis_index(axis) == 0
    low, high = jnp.where(first, x, other), jnp.where(first, other, x)
    return jnp.concatenate([low, high], axis=dim)


def with_rims(x, select):
    tiles = x.shape[0] - 2 * REACH
    channels = x.shape[3]
    sides = jnp.concatenate([x[:, 0], x[:, P_SIZE - 1], x[:, :, 0], x[:, :, P_SIZE - 1]], axis=1)
    near = jnp.concatenate([sides[i : i + tiles] for i in range(2 * REACH + 1)], axis=1)
    border = jnp.einsum("tbs,tsc->tbc", select, near, preferred_element_type=jnp.float32).astype(jnp.bfloat16)
    side = P_SIZE + 2
    above = border[:, :side].reshape(tiles, 1, side, channels)
    below = border[:, side : 2 * side].reshape(tiles, 1, side, channels)
    left = border[:, 2 * side : 2 * side + P_SIZE].reshape(tiles, P_SIZE, 1, channels)
    right = border[:, 2 * side + P_SIZE :].reshape(tiles, P_SIZE, 1, channels)
    middle = jnp.concatenate([left, x[REACH : REACH + tiles], right], axis=2)
    return jnp.concatenate([above, middle, below], axis=1)


def conv(padded, kernel):
    summed = lax.conv_general_dilated(
        padded,
        kernel.reshape(3, 3, kernel.shape[1], kernel.shape[2]),
        (1, 1),
        "VALID",
        dimension_numbers=("NHWC", "HWOI", "NHWC"),
        preferred_element_type=jnp.float32,
    )
    return jax.nn.gelu(summed, approximate=False).astype(jnp.bfloat16)


def on_device(
    analysis,
    send_rows,
    send_count,
    corner_slot,
    corner_weight,
    beside,
    quarter_turns,
    kernel_one,
    kernel_two,
    kernel_three,
):
    shards = lax.axis_size("tile")
    groups = lax.axis_size("chan")
    both = ("tile", "chan")
    tiles_here = corner_slot.shape[1]
    pixels = corner_slot.shape[2]
    near_count, capacity = send_rows.shape[1:]
    total_tiles = tiles_here * shards
    per_group = tiles_here // groups
    mine = lax.axis_index("chan") * per_group

    picked = jnp.take(analysis, send_rows.reshape(-1), axis=1, mode="clip")
    live = jnp.arange(capacity)[None, :] < send_count[0][:, None]
    picked = jnp.where(live.reshape(-1)[None, :], picked, jnp.zeros((), picked.dtype))
    wide = REACH * (LAYERS - 1)
    tile_ids = lax.axis_index("tile") * tiles_here + jnp.arange(tiles_here)
    steps = jnp.remainder(beside - tile_ids[:, None] + REACH, total_tiles)
    near = steps * 4 + quarter_turns
    riders = {1: near[tiles_here - wide :], -1: near[:wide]}
    came_along = {}
    blocks = []
    for d in range(near_count):
        hop = d - REACH
        piece = picked[:, d * capacity : (d + 1) * capacity]
        if hop in riders:
            rider = riders[hop].astype(piece.dtype).reshape(piece.shape[0], -1)
            piece = from_behind(jnp.concatenate([piece, rider], axis=1), "tile", hop)
            came_along[hop] = piece[:, capacity:].reshape(wide, -1).astype(jnp.int32)
            piece = piece[:, :capacity]
        elif hop != 0:
            piece = from_behind(piece, "tile", hop)
        blocks.append(piece)
    arrived = gathered(jnp.concatenate(blocks, axis=1), "chan", 0)

    sizes = [k.shape[2] for k in (kernel_one, kernel_two, kernel_three)]
    joined = jnp.concatenate([kernel_one, kernel_two, kernel_three], axis=2)
    joined = gathered(joined, "chan", 1)
    cuts = np.cumsum([0] + sizes)
    kernels = [joined[:, :, cuts[i] : cuts[i + 1]] for i in range(LAYERS)]

    near = jnp.concatenate([came_along[1], near, came_along[-1]], axis=0)
    near = lax.dynamic_slice_in_dim(near, mine, per_group + 2 * wide, 0)
    steps, turns = near // 4, near % 4
    heading, anchor = border_tables()
    near_step = jnp.stack([steps[:, k] for k in heading], axis=1)
    near_turn = jnp.stack([turns[:, k] for k in heading], axis=1)
    source = near_step * 64 + jnp.remainder(anchor[None, :] - near_turn * (P_SIZE - 1), 4 * P_SIZE - 4)
    select = (source[:, :, None] == side_keys()[None, None, :]).astype(jnp.bfloat16)

    base = lax.dynamic_slice_in_dim(corner_slot[0], mine, per_group, 0).reshape(-1)
    weights = lax.dynamic_slice_in_dim(corner_weight, mine, per_group, 1).reshape(4, -1)
    base = base.astype(jnp.int16)
    slots = jnp.arange(near_count * capacity, dtype=jnp.int16)[:, None]
    coarse = lax.reduce_precision(weights, 8, 7)
    x = jnp.zeros((), jnp.float32)
    for part in (coarse, weights - coarse):
        part = part.astype(jnp.bfloat16)
        spread = jnp.zeros((), jnp.bfloat16)
        for j in range(4):
            spread = jnp.where(slots == (base + jnp.int16(j))[None, :], part[j][None, :], spread)
        x = x + lax.dot_general(spread, arrived, (((0,), (1,)), ((), ())), preferred_element_type=jnp.float32)
    x = x.astype(jnp.bfloat16).reshape(per_group, P_SIZE, P_SIZE, arrived.shape[0])

    reach = 2 * REACH
    early, late = around(x, REACH * LAYERS, both)
    x = conv(with_rims(jnp.concatenate([early, x, late], axis=0), select), kernels[0])
    padded = with_rims(x, select[REACH : REACH + per_group + reach])

    def last(x, select):
        y = conv(with_rims(x, select), kernels[2])
        return jnp.transpose(y.reshape(y.shape[0], pixels, y.shape[3]), (2, 0, 1))

    select = select[reach : reach + per_group]
    if groups != 2:
        x = last(conv(padded, kernels[1]), select)
        return lax.all_to_all(x, "chan", split_axis=0, concat_axis=1, tiled=True)
    first = lax.axis_index("chan") == 0
    kept, came = [], []
    half = per_group // 2
    x = None
    for k in range(2):
        if k == 0:
            x = conv(padded[: half + reach], kernels[1])
        else:
            rest = conv(padded[half + reach :], kernels[1])
            x = jnp.concatenate([x[half:], rest], axis=0)
        y = last(x, select[k * half : (k + 1) * half])
        share = y.shape[0] // 2
        kept.append(jnp.where(first, y[:share], y[share:]))
        sent = jnp.where(first, y[share:], y[:share])
        if k == 0:
            sent, padded = lax.optimization_barrier((sent, padded))
        came.append(lax.ppermute(sent, "chan", [(0, 1), (1, 0)]))
    kept, came = jnp.concatenate(kept, axis=1), jnp.concatenate(came, axis=1)
    return jnp.concatenate([jnp.where(first, kept, came), jnp.where(first, came, kept)], axis=1)


def solution(mesh):
    return jax.shard_map(
        on_device,
        mesh=mesh,
        in_specs=(
            P("chan", "tile"),
            P("tile", None, None),
            P("tile", None),
            P(None, "tile", None),
            P(None, "tile", None),
            P("tile", None),
            P("tile", None),
            P(None, "chan", None),
            P(None, "chan", None),
            P(None, "chan", None),
        ),
        out_specs=P("chan", "tile", None),
        check_vma=False,
    )
```
